256 devices in a mesh: dp: 16 (over y_hi, x, core), cent: 8 (over z), rep: 2 (over y_lo).
Axes of the slice: x: 4, y: 4 (y_hi: 2, y_lo: 2; y = y_hi * 2 + y_lo), z: 8, core: 2. Of those that a mesh axis runs over, the one named last changes fastest.
Arguments:
- points: bfloat16 [16384, 1024], P('dp'), may hold values from -6 to 6
- centroids: bfloat16 [8, 4096, 1024], P('rep', 'cent'), may hold values from -1.5 to 1.5
- counts: int32 [8, 16384], P('rep', 'dp'), may hold values from 0 to 5, as said below
Outputs:
- updated: bfloat16 [8, 4096, 1024], P('rep', 'cent', 'dp')
- bagged_score: float32 [16384], P('dp')
The draws below stay inside these ranges and needn't reach their ends.
Inputs may be any that keep to these rules, and one draw needn't show every extreme that they name: `counts`: in every replicate some point has count 5.
All inputs are finite; a program needn't handle non-finite values.
Results may differ from the reference program's by a relative error of at most 0.0045.
Values sent between devices are 32-bit elements; how exact they have to be, the bound alone decides.
A program may use at most 64 MiB of HBM per device.

```python
import math
import jax
import jax.numpy as jnp
import numpy as np
from jax import lax

D = 1024
K = 4096
REPS = 8
POINTS = 16384


def drawn_layout():
    replica = np.repeat(np.arange(REPS), 8)
    member = np.tile(np.arange(8), REPS)
    target = 110.0 + 20.0 * member
    amplitude = np.minimum(np.floor(16.0 * (target / D + 1.125) / 1.5 + 0.5) / 16.0, 6.0)
    grid = np.arange(-12, 13) / 8.0
    altered = np.zeros(member.shape[0])
    for index in range(member.shape[0]):
        gaps = (1.5 - grid) * (amplitude[index] - (1.5 + grid) / 2.0)
        altered[index] = grid[np.argmin(np.abs(gaps - 2.0))]
    return (replica, amplitude.astype(np.float32), altered.astype(np.float32))


def drawn_points(key):
    order = jax.random.permutation(jax.random.fold_in(key, 16), POINTS)
    return order[:REPS * 8]


def pick_rows(branch_key):
    return jax.random.permutation(branch_key, K // 2)[:8]


def drawn_rows(key):
    branch_keys = jax.random.split(jax.random.fold_in(key, 17), REPS)
    halves = jax.vmap(pick_rows)(branch_keys)
    first_row = 2 * halves.reshape(-1)
    return (first_row, first_row + 1)


def planted_signs(key):
    bits = jax.random.bernoulli(jax.random.fold_in(key, 15), 0.5, (REPS * 8, D))
    return jnp.where(bits, 1.0, -1.0).astype(jnp.float32)


def base_points(key):
    inner = jax.random.fold_in(key, 11)
    source = jnp.clip(jax.random.normal(inner, (POINTS, D), jnp.float32), -6.0, 6.0)
    replica, amplitude, altered = drawn_layout()
    picked = drawn_points(key)
    signs = planted_signs(key)
    return source.at[picked].set(jnp.asarray(amplitude)[:, None] * signs)


def draw_points(key, part):
    return base_points(key).astype(jnp.bfloat16)


def draw_centroids(key, part):
    noise = 0.1 * jnp.clip(jax.random.normal(jax.random.fold_in(key, 12), (REPS, K, D), jnp.float32), -6.0, 6.0)
    replica, amplitude, altered = drawn_layout()
    first_row, second_row = drawn_rows(key)
    signs = planted_signs(key)
    first_values = 1.5 * signs
    second_values = first_values.at[:, 0].set(jnp.asarray(altered) * signs[:, 0])
    noise = noise.at[replica, first_row].set(first_values)
    noise = noise.at[replica, second_row].set(second_values)
    return noise.astype(jnp.bfloat16)


def draw_counts(key, part):
    trials = jax.random.randint(jax.random.fold_in(key, 13), (16, REPS, POINTS), 0, 16)
    drawn = jnp.minimum(jnp.sum((trials == 0).astype(jnp.int32), axis=0), 5)
    spots = jax.random.randint(jax.random.fold_in(key, 14), (REPS,), 0, POINTS)
    return drawn.at[jnp.arange(REPS), spots].set(5)


def setup_inputs(seed: int = 0) -> dict:
    key_list = jax.random.split(jax.random.key(seed), 4)
    return {
        "points": draw_points(jax.random.fold_in(key_list[3], 71), 0),
        "centroids": draw_centroids(jax.random.fold_in(key_list[3], 71), 0),
        "counts": draw_counts(jax.random.fold_in(key_list[3], 71), 0),
    }


prior_weight = 1.0


def reference(points, centroids, counts):
    def one_replicate(pair):
        center, weight = pair
        squares = jnp.sum(jnp.square(center.astype(jnp.float32)), axis=1)
        logits = jnp.dot(points, center.T, preferred_element_type=jnp.float32) - 0.5 * squares[None, :]
        row_top = jnp.max(logits, axis=1, keepdims=True)
        expo = jnp.exp(logits - row_top)
        row_total = jnp.sum(expo, axis=1, keepdims=True)
        weighted = (expo / row_total * weight[:, None].astype(jnp.float32)).astype(jnp.bfloat16)
        moment_sums = jnp.dot(weighted.T, points, preferred_element_type=jnp.float32)
        cluster_mass = jnp.sum(weighted.astype(jnp.float32), axis=0)
        updated = ((moment_sums + prior_weight * center.astype(jnp.float32)) / (cluster_mass + prior_weight)[:, None]).astype(jnp.bfloat16)
        log_total = row_top[:, 0] + jnp.log(row_total[:, 0])
        return updated, log_total

    updated, log_total = lax.map(one_replicate, (centroids, counts))
    bagged_score = jnp.sum(log_total, axis=0) / REPS - math.log(K)
    return updated, bagged_score
```

```python
import math

import jax
import jax.numpy as jnp
from jax import lax
from jax.experimental import pallas as pl
from jax.experimental.pallas import tpu as pltpu
from jax.sharding import PartitionSpec as P

MESH = pl.DeviceIdType.MESH
F32 = jnp.float32
REPS = 4
NK = 512
HALF = 256
D = 1024
N = 1024
RA = 144
RB = HALF - RA
HB = RB // 2
NT = 256
OFFS = (2, 1, 3, 0)
prior_weight = 1.0

REL_P, REL_M, PLA_P, PLA_M, AUG_P, AUG_M, Y_A, Y_B, BREL_P, BREL_M, BPLA_P, BPLA_M, BAUG_P, BAUG_M = range(14)


def pack(top, low):
    first = lax.broadcasted_iota(jnp.int32, top.shape, 1) < 64
    swapped = pltpu.roll(jnp.where(first, low, top), 64, 1)
    return jnp.where(first, top, swapped), jnp.where(first, swapped, low)


def kernel(
    p_hbm, c_hbm, n_hbm, u_ref, b_ref,
    p_v, c_v, n_v, e_v, w_v, hs_v, st, mp, cr, sa, sb,
    ra_m, ra_p, da_m, da_p, ya, yb, rb_m, rb_p, db_m, db_p, mass, lt,
    ld, zs, zr, cs, crs, xs, xr, ms, mr, ls, lr,
):
    p = lax.axis_index("dp")
    z = lax.axis_index("cent")
    l = lax.axis_index("rep")
    c = p % 2
    x = (p // 2) % 4
    yh = p // 8
    sib = (p + 1 - 2 * c, z, l)
    xp = (yh * 8 + ((x + 1) % 4) * 2 + c, z, l)
    xm = (yh * 8 + ((x + 3) % 4) * 2 + c, z, l)
    y2 = ((1 - yh) * 8 + x * 2 + c, z, l)
    other = (p, z, 1 - l)

    loads = [pltpu.make_async_copy(p_hbm, p_v, ld.at[0])]
    loads.append(pltpu.make_async_copy(n_hbm, n_v, ld.at[1]))
    for r in range(REPS):
        loads.append(pltpu.make_async_copy(c_hbm.at[r], c_v.at[r], ld.at[2 + r]))
    for i in (2, 0, 3, 4, 5, 1):
        loads[i].start()

    barrier = pltpu.get_barrier_semaphore()
    for j in range(1, 16):
        pl.semaphore_signal(barrier, inc=1, device_id=((p + j) % 16, z, l), device_id_type=MESH)
    for j in range(1, 8):
        pl.semaphore_signal(barrier, inc=1, device_id=(p, (z + j) % 8, l), device_id_type=MESH)
    pl.semaphore_signal(barrier, inc=1, device_id=other, device_id_type=MESH)

    sent = []

    def send(src, dst, ssem, rsem, dev):
        copy = pltpu.make_async_remote_copy(
            src_ref=src, dst_ref=dst, send_sem=ssem, recv_sem=rsem, device_id=dev, device_id_type=MESH
        )
        copy.start()
        sent.append(copy)
        return copy

    def logits(r):
        loads[2 + r].wait()
        if r == 0:
            loads[0].wait()
        for i in range(0, NK, 64):
            block = c_v[r, i : i + 64, :].astype(F32)
            hs_v[i : i + 64, :] = jnp.broadcast_to(
                0.5 * jnp.sum(block * block, axis=1, keepdims=True), (64, 128)
            )

        def tile(t, carry):
            cols = pl.ds(pl.multiple_of(t * NT, NT), NT)
            e_v[r, :, cols] = lax.dot_general(
                c_v[r], p_v[cols, :], (((1,), (1,)), ((), ())), preferred_element_type=F32
            )
            top = None
            for i in range(0, NK, 64):
                half = hs_v[i : i + 64, :]
                block = e_v[r, i : i + 64, cols] - jnp.concatenate([half, half], axis=1)
                e_v[r, i : i + 64, cols] = block
                part = jnp.max(block.reshape(8, 8, NT), axis=0)
                top = part if top is None else jnp.maximum(top, part)
            top = jnp.max(top, axis=0, keepdims=True)
            total = None
            for i in range(0, NK, 64):
                block = jnp.exp(e_v[r, i : i + 64, cols] - top)
                e_v[r, i : i + 64, cols] = block
                part = jnp.sum(block.reshape(8, 8, NT), axis=0)
                total = part if total is None else total + part
            st[r, z, 0:1, cols] = top
            st[r, z, 1:2, cols] = jnp.sum(total, axis=0, keepdims=True)
            return carry

        lax.fori_loop(0, N // NT, tile, 0)

    zc = {}

    def send_stats(r):
        for j in range(1, 8):
            zc[r, j] = send(st.at[r, z], st.at[r, z], zs.at[r, j], zr.at[r, j], (p, (z + j) % 8, l))

    cc = {}

    def moments(r):
        for j in range(1, 8):
            zc[r, j].wait_recv()
        top = st[r, 0, 0:1, :]
        for j in range(1, 8):
            top = jnp.maximum(top, st[r, j, 0:1, :])
        total = jnp.zeros_like(top)
        for j in range(8):
            total += st[r, j, 1:2, :] * jnp.exp(st[r, j, 0:1, :] - top)
        scale = jnp.exp(st[r, z, 0:1, :] - top) / total * n_v[r : r + 1, :].astype(F32)
        log_total = top + jnp.log(total)
        if r == 0:
            lt[l, :, :] = log_total
        else:
            lt[l, :, :] += log_total
        for i in range(0, NK, 32):
            w_v[i : i + 32, :] = (e_v[r, i : i + 32, :] * scale).astype(jnp.bfloat16)
        for g in range(4):
            xx = (x + OFFS[g]) % 4
            lo = pl.ds(pl.multiple_of(xx * 128, 128), 128)
            hi = pl.ds(pl.multiple_of(512 + xx * 128, 128), 128)
            block = jnp.concatenate([p_v[:, lo], p_v[:, hi]], axis=1)
            out = jnp.dot(w_v[...], block, preferred_element_type=F32)
            for h in range(2):
                part = out[:, h * 128 : (h + 1) * 128]
                zero, one = pack(part[:HALF], part[HALF:])
                mp[r, 0, xx, h, :, :] = zero
                mp[r, 1, xx, h, :, :] = one
            cc[r, g] = send(mp.at[r, 1 - c, xx], cr.at[r, xx], cs.at[r, g], crs.at[r, g], sib)
        sums = jnp.dot(w_v[...], jnp.ones((N, 128), jnp.bfloat16), preferred_element_type=F32)
        eye = lax.broadcasted_iota(jnp.int32, (128, 128), 0) == lax.broadcasted_iota(
            jnp.int32, (128, 128), 1
        )
        for g in range(4):
            mass[p, r * 4 + g : r * 4 + g + 1, :] = jnp.sum(
                jnp.where(eye, sums[g * 128 : (g + 1) * 128], 0.0), axis=0, keepdims=True
            )

    xc = {}

    def xsend(r, i, src, dst, dev):
        xc[r, i] = send(src, dst, xs.at[r, i], xr.at[r, i], dev)

    x_opp, x_next, x_prev = (x + 2) % 4, (x + 1) % 4, (x + 3) % 4

    def stage1(r):
        for g in range(4):
            xx = (x + OFFS[g]) % 4
            cc[r, g].wait_recv()
            for h in range(2):
                sa[r, xx, h, :, :] = mp[r, c, xx, h, :RA, :] + cr[r, xx, h, :RA, :]
                sb[r, h, xx, :, :] = mp[r, c, xx, h, RA:, :] + cr[r, xx, h, RA:, :]
            if g == 0:
                xsend(r, REL_P, sa.at[r, x_opp, 0], ra_m.at[r], xp)
                xsend(r, REL_M, sa.at[r, x_opp, 1], ra_p.at[r], xm)
            if g == 1:
                xsend(r, PLA_P, sa.at[r, x_next, 1], da_m.at[r, 1], xp)
            if g == 2:
                xsend(r, PLA_M, sa.at[r, x_prev, 0], da_p.at[r, 0], xm)
        xsend(r, Y_B, sb.at[r, 1 - yh], yb.at[r], y2)

    def stage2(r):
        xc[r, REL_P].wait_recv()
        sa[r, x_next, 0, :, :] += ra_m[r]
        xsend(r, AUG_P, sa.at[r, x_next, 0], da_m.at[r, 0], xp)
        xc[r, REL_M].wait_recv()
        sa[r, x_prev, 1, :, :] += ra_p[r]
        xsend(r, AUG_M, sa.at[r, x_prev, 1], da_p.at[r, 1], xm)
        xc[r, Y_B].wait_recv()
        sb[r, yh, x_opp, :, :] += yb[r, x_opp]
        xsend(r, BREL_P, sb.at[r, yh, x_opp, pl.ds(0, HB)], rb_m.at[r], xp)
        xsend(r, BREL_M, sb.at[r, yh, x_opp, pl.ds(HB, HB)], rb_p.at[r], xm)
        sb[r, yh, x_next, :, :] += yb[r, x_next]
        xsend(r, BPLA_P, sb.at[r, yh, x_next, pl.ds(HB, HB)], db_m.at[r, pl.ds(HB, HB)], xp)
        sb[r, yh, x_prev, :, :] += yb[r, x_prev]
        xsend(r, BPLA_M, sb.at[r, yh, x_prev, pl.ds(0, HB)], db_p.at[r, pl.ds(0, HB)], xm)

    def stage3(r):
        for i in (PLA_P, PLA_M, AUG_P, AUG_M):
            xc[r, i].wait_recv()
        for h in range(2):
            sa[r, x, h, :, :] += da_m[r, h] + da_p[r, h]
        xsend(r, Y_A, sa.at[r, x, 1 - yh], ya.at[r], y2)
        xc[r, BREL_P].wait_recv()
        sb[r, yh, x_next, :HB, :] += rb_m[r]
        xsend(r, BAUG_P, sb.at[r, yh, x_next, pl.ds(0, HB)], db_m.at[r, pl.ds(0, HB)], xp)
        xc[r, BREL_M].wait_recv()
        sb[r, yh, x_prev, HB:, :] += rb_p[r]
        xsend(r, BAUG_M, sb.at[r, yh, x_prev, pl.ds(HB, HB)], db_p.at[r, pl.ds(HB, HB)], xm)

    mc = {}

    def send_mass():
        for j in range(1, 16):
            mc[j] = send(mass.at[p], mass.at[p], ms.at[j], mr.at[j], ((p + j) % 16, z, l))
        mc[0] = send(lt.at[l], lt.at[l], ls, lr, other)

    masses = []

    def receive_mass():
        for j in range(1, 16):
            mc[j].wait_recv()
        total = mass[0]
        for j in range(1, 16):
            total += mass[j]
        masses.append(total)
        mc[0].wait_recv()
        b_ref[...] = (lt[0] + lt[1]) / 8.0 - math.log(4096)

    def stage4(r):
        q = pl.ds(pl.multiple_of((yh * 4 + x) * 128, 128), 128)
        total = masses[0]
        row = lax.broadcasted_iota(jnp.int32, (128, 128), 0)
        cols = []
        for i in range(2):
            a = total[r * 4 + i : r * 4 + i + 1, :]
            b = total[r * 4 + 2 + i : r * 4 + 3 + i, :]
            cols.append(jnp.where(row < 64, a, b).T)
        weight = jnp.concatenate(cols, axis=0) + prior_weight
        zero, one = pack(c_v[r, :HALF, q].astype(F32), c_v[r, HALF:, q].astype(F32))
        own = prior_weight * jnp.where(jnp.full((HALF, 128), c, jnp.int32) == 0, zero, one)
        for i in (BPLA_P, BPLA_M, BAUG_P, BAUG_M):
            xc[r, i].wait_recv()
        low = sb[r, yh, x] + yb[r, x] + db_m[r] + db_p[r]
        u_ref[r, RA:, :] = ((low + own[RA:]) / weight[RA:]).astype(jnp.bfloat16)
        xc[r, Y_A].wait_recv()
        high = sa[r, x, yh] + ya[r]
        u_ref[r, :RA, :] = ((high + own[:RA]) / weight[:RA]).astype(jnp.bfloat16)

    logits(0)
    pl.semaphore_wait(barrier, 23)
    send_stats(0)
    for r in range(1, REPS):
        logits(r)
        send_stats(r)
    loads[1].wait()
    moments(0)
    stage1(0)
    moments(1)
    stage1(1)
    stage2(0)
    moments(2)
    stage1(2)
    stage2(1)
    stage3(0)
    moments(3)
    send_mass()
    stage1(3)
    stage2(2)
    stage3(1)
    receive_mass()
    stage4(0)
    stage2(3)
    stage3(2)
    stage4(1)
    stage3(3)
    stage4(2)
    stage4(3)
    for copy in sent:
        copy.wait_send()


def shards(points, centroids, counts):
    dma = pltpu.SemaphoreType.DMA
    packed, bagged = pl.pallas_call(
        kernel,
        out_shape=(
            jax.ShapeDtypeStruct((REPS, HALF, 128), jnp.bfloat16),
            jax.ShapeDtypeStruct((1, N), F32),
        ),
        in_specs=[pl.BlockSpec(memory_space=pl.ANY)] * 3,
        out_specs=[pl.BlockSpec(memory_space=pltpu.VMEM)] * 2,
        scratch_shapes=[
            pltpu.VMEM((N, D), jnp.bfloat16),
            pltpu.VMEM((REPS, NK, D), jnp.bfloat16),
            pltpu.VMEM((REPS, N), jnp.int32),
            pltpu.VMEM((REPS, NK, N), F32),
            pltpu.VMEM((NK, N), jnp.bfloat16),
            pltpu.VMEM((NK, 128), F32),
            pltpu.VMEM((REPS, 8, 2, N), F32),
            pltpu.VMEM((REPS, 2, 4, 2, HALF, 128), F32),
            pltpu.VMEM((REPS, 4, 2, HALF, 128), F32),
            pltpu.VMEM((REPS, 4, 2, RA, 128), F32),
            pltpu.VMEM((REPS, 2, 4, RB, 128), F32),
            pltpu.VMEM((REPS, RA, 128), F32),
            pltpu.VMEM((REPS, RA, 128), F32),
            pltpu.VMEM((REPS, 2, RA, 128), F32),
            pltpu.VMEM((REPS, 2, RA, 128), F32),
            pltpu.VMEM((REPS, RA, 128), F32),
            pltpu.VMEM((REPS, 4, RB, 128), F32),
            pltpu.VMEM((REPS, HB, 128), F32),
            pltpu.VMEM((REPS, HB, 128), F32),
            pltpu.VMEM((REPS, RB, 128), F32),
            pltpu.VMEM((REPS, RB, 128), F32),
            pltpu.VMEM((16, 4 * REPS, 128), F32),
            pltpu.VMEM((2, 1, N), F32),
            dma((2 + REPS,)),
            dma((REPS, 8)),
            dma((REPS, 8)),
            dma((REPS, 4)),
            dma((REPS, 4)),
            dma((REPS, 14)),
            dma((REPS, 14)),
            dma((16,)),
            dma((16,)),
            dma,
            dma,
        ],
        compiler_params=pltpu.CompilerParams(
            collective_id=0, has_side_effects=True, vmem_limit_bytes=56 * 1024 * 1024
        ),
    )(points, centroids, counts)
    updated = packed.reshape(REPS, HALF, 2, 64).transpose(0, 2, 1, 3).reshape(REPS, NK, 64)
    return updated, bagged.reshape(N)


def solution(mesh):
    return jax.shard_map(
        shards,
        mesh=mesh,
        in_specs=(P("dp", None), P("rep", "cent", None), P("rep", "dp")),
        out_specs=(P("rep", "cent", "dp"), P("dp")),
        check_vma=False,
    )
```

```python
import math

import jax
import jax.numpy as jnp
from jax import lax
from jax.experimental import pallas as pl
from jax.experimental.pallas import tpu as pltpu
from jax.sharding import PartitionSpec as P

MESH = pl.DeviceIdType.MESH
F32 = jnp.float32
REPS = 4
NK = 512
HALF = 256
D = 1024
N = 1024
RA = 144
RB = HALF - RA
HB = RB // 2
NT = 256
LAG = 3
OFFS = (2, 1, 3, 0)
prior_weight = 1.0

REL_P, REL_M, PLA_P, PLA_M, AUG_P, AUG_M, Y_A, BREL_P, BREL_M, BPLA_P, BPLA_M, BAUG_P, BAUG_M, Y_B = range(14)
EXCHANGES = Y_B + 4

EARLY = {11: [("aug_a", 0)], 15: [("aug_a", 1)]}
LATE = [
    ("rel_b", 0), ("aug_a", 2), ("y_a", 0), ("rel_b", 1), ("aug_a", 3), ("aug_b", 0), ("y_a", 1), ("rel_b", 2),
    ("aug_b", 1), ("y_a", 2), ("rel_b", 3), ("aug_b", 2), ("y_a", 3), ("finish", 0), ("finish", 1), ("aug_b", 3),
    ("finish", 2), ("finish", 3),
]


def pack(top, low):
    first = lax.broadcasted_iota(jnp.int32, top.shape, 1) < 64
    swapped = pltpu.roll(jnp.where(first, low, top), 64, 1)
    return jnp.where(first, top, swapped), jnp.where(first, swapped, low)


def kernel(
    p_hbm, c_hbm, n_hbm, u_ref, b_ref,
    p_v, c_v, n_v, e_v, w_v, hs_v, sc_v, st, mp, cr, sa, sb,
    ra_m, ra_p, da_m, da_p, ya, yb, rb_m, rb_p, db_m, db_p, mass, lt,
    ld, zs, zr, cs, crs, xs, xr, ms, mr, ls, lr,
):
    p = lax.axis_index("dp")
    z = lax.axis_index("cent")
    l = lax.axis_index("rep")
    c = p % 2
    x = (p // 2) % 4
    yh = p // 8
    sib = (p + 1 - 2 * c, z, l)
    xp = (yh * 8 + ((x + 1) % 4) * 2 + c, z, l)
    xm = (yh * 8 + ((x + 3) % 4) * 2 + c, z, l)
    y2 = ((1 - yh) * 8 + x * 2 + c, z, l)
    other = (p, z, 1 - l)

    loads = [pltpu.make_async_copy(p_hbm, p_v, ld.at[0])]
    loads.append(pltpu.make_async_copy(n_hbm, n_v, ld.at[1]))
    for r in range(REPS):
        loads.append(pltpu.make_async_copy(c_hbm.at[r], c_v.at[r], ld.at[2 + r]))
    for i in (2, 0, 3, 4, 5, 1):
        loads[i].start()

    barrier = pltpu.get_barrier_semaphore()
    for j in range(1, 16):
        pl.semaphore_signal(barrier, inc=1, device_id=((p + j) % 16, z, l), device_id_type=MESH)
    for j in range(1, 8):
        pl.semaphore_signal(barrier, inc=1, device_id=(p, (z + j) % 8, l), device_id_type=MESH)
    pl.semaphore_signal(barrier, inc=1, device_id=other, device_id_type=MESH)

    sent = []

    def send(src, dst, ssem, rsem, dev):
        copy = pltpu.make_async_remote_copy(
            src_ref=src, dst_ref=dst, send_sem=ssem, recv_sem=rsem, device_id=dev, device_id_type=MESH
        )
        copy.start()
        sent.append(copy)
        return copy

    def logits(r):
        loads[2 + r].wait()
        if r == 0:
            loads[0].wait()
        for i in range(0, NK, 64):
            block = c_v[r, i : i + 64, :].astype(F32)
            hs_v[i : i + 64, :] = jnp.broadcast_to(
                0.5 * jnp.sum(block * block, axis=1, keepdims=True), (64, 128)
            )

        for t in range(0, N, NT):
            cols = slice(t, t + NT)
            half = hs_v[...]
            tile = lax.dot_general(
                c_v[r], p_v[cols, :], (((1,), (1,)), ((), ())), preferred_element_type=F32
            ) - jnp.concatenate([half, half], axis=1)
            top = jnp.max(tile, axis=0, keepdims=True)
            tile = jnp.exp(tile - top)
            e_v[r, :, cols] = tile
            st[r, z, 0:1, cols] = top
            st[r, z, 1:2, cols] = jnp.sum(tile, axis=0, keepdims=True)

    zc = {}

    def send_stats(r):
        for j in range(1, 8):
            zc[r, j] = send(st.at[r, z], st.at[r, z], zs.at[r, j], zr.at[r, j], (p, (z + j) % 8, l))

    cc = {}

    def scale(r):
        for j in range(1, 8):
            zc[r, j].wait_recv()
        top = st[r, 0, 0:1, :]
        for j in range(1, 8):
            top = jnp.maximum(top, st[r, j, 0:1, :])
        total = jnp.zeros_like(top)
        for j in range(8):
            total += st[r, j, 1:2, :] * jnp.exp(st[r, j, 0:1, :] - top)
        sc_v[r, :, :] = jnp.exp(st[r, z, 0:1, :] - top) / total * n_v[r : r + 1, :].astype(F32)
        log_total = top + jnp.log(total)
        if r == 0:
            lt[l, :, :] = log_total
        else:
            lt[l, :, :] += log_total

    def weights(r, g):
        factor = sc_v[r]
        parts = []
        for i in range(g * 128, g * 128 + 128, 32):
            w = (e_v[r, i : i + 32, :] * factor).astype(jnp.bfloat16)
            w_v[r % 2, i : i + 32, :] = w
            w = w.astype(F32)
            part = w[:, :128]
            for k in range(128, N, 128):
                part = part + w[:, k : k + 128]
            parts.append(part)
        part = jnp.concatenate(parts, axis=0).T
        mass[p, r * 4 + g : r * 4 + g + 1, :] = jnp.sum(part, axis=0, keepdims=True)

    def moments(r, g):
        xx = (x + OFFS[g]) % 4
        lo = pl.ds(pl.multiple_of(xx * 128, 128), 128)
        hi = pl.ds(pl.multiple_of(512 + xx * 128, 128), 128)
        block = jnp.concatenate([p_v[:, lo], p_v[:, hi]], axis=1)
        out = jnp.dot(w_v[r % 2], block, preferred_element_type=F32)
        for h in range(2):
            part = out[:, h * 128 : (h + 1) * 128]
            zero, one = pack(part[:HALF], part[HALF:])
            mp[r, 0, xx, h, :, :] = zero
            mp[r, 1, xx, h, :, :] = one

    cc = {}

    def send_moments(r, g):
        xx = (x + OFFS[g]) % 4
        cc[r, g] = send(mp.at[r, 1 - c, xx], cr.at[r, xx], cs.at[r, g], crs.at[r, g], sib)

    xc = {}

    def xsend(r, i, src, dst, dev):
        xc[r, i] = send(src, dst, xs.at[r, i], xr.at[r, i], dev)

    x_opp, x_next, x_prev = (x + 2) % 4, (x + 1) % 4, (x + 3) % 4

    def own_centroids(r):
        q = pl.ds(pl.multiple_of((yh * 4 + x) * 128, 128), 128)
        zero, one = pack(c_v[r, :HALF, q].astype(F32), c_v[r, HALF:, q].astype(F32))
        return prior_weight * jnp.where(jnp.full((HALF, 128), c, jnp.int32) == 0, zero, one)

    def sum_cores(r, g):
        xx = (x + OFFS[g]) % 4
        for h in range(2):
            sa[r, xx, h, :, :] = mp[r, c, xx, h, :RA, :] + cr[r, xx, h, :RA, :]
            sb[r, h, xx, :, :] = mp[r, c, xx, h, RA:, :] + cr[r, xx, h, RA:, :]
        if g == 3:
            own = own_centroids(r)
            sa[r, x, yh, :, :] += own[:RA]
            sb[r, yh, x, :, :] += own[RA:]

    def send_cores(r, g):
        if g == 0:
            xsend(r, REL_P, sa.at[r, x_opp, 0], ra_m.at[r], xp)
            xsend(r, REL_M, sa.at[r, x_opp, 1], ra_p.at[r], xm)
        if g == 1:
            xsend(r, PLA_P, sa.at[r, x_next, 1], da_m.at[r, 1], xp)
        if g == 2:
            xsend(r, PLA_M, sa.at[r, x_prev, 0], da_p.at[r, 0], xm)
        xx = (x + OFFS[g]) % 4
        xsend(r, Y_B + g, sb.at[r, 1 - yh, xx], yb.at[r, xx], y2)

    def aug_a(r):
        xc[r, REL_P].wait_recv()
        sa[r, x_next, 0, :, :] += ra_m[r]
        xsend(r, AUG_P, sa.at[r, x_next, 0], da_m.at[r, 0], xp)
        xc[r, REL_M].wait_recv()
        sa[r, x_prev, 1, :, :] += ra_p[r]
        xsend(r, AUG_M, sa.at[r, x_prev, 1], da_p.at[r, 1], xm)

    def rel_b(r):
        xc[r, Y_B].wait_recv()
        sb[r, yh, x_opp, :, :] += yb[r, x_opp]
        xsend(r, BREL_P, sb.at[r, yh, x_opp, pl.ds(0, HB)], rb_m.at[r], xp)
        xsend(r, BREL_M, sb.at[r, yh, x_opp, pl.ds(HB, HB)], rb_p.at[r], xm)
        xc[r, Y_B + 1].wait_recv()
        sb[r, yh, x_next, :, :] += yb[r, x_next]
        xsend(r, BPLA_P, sb.at[r, yh, x_next, pl.ds(HB, HB)], db_m.at[r, pl.ds(HB, HB)], xp)
        xc[r, Y_B + 2].wait_recv()
        sb[r, yh, x_prev, :, :] += yb[r, x_prev]
        xsend(r, BPLA_M, sb.at[r, yh, x_prev, pl.ds(0, HB)], db_p.at[r, pl.ds(0, HB)], xm)
        xc[r, Y_B + 3].wait_recv()
        sb[r, yh, x, :, :] += yb[r, x]

    def y_a(r):
        for i in (PLA_P, PLA_M, AUG_P, AUG_M):
            xc[r, i].wait_recv()
        sa[r, x, 1 - yh, :, :] += da_m[r, 1 - yh] + da_p[r, 1 - yh]
        xsend(r, Y_A, sa.at[r, x, 1 - yh], ya.at[r], y2)
        sa[r, x, yh, :, :] += da_m[r, yh] + da_p[r, yh]

    def aug_b(r):
        xc[r, BREL_P].wait_recv()
        sb[r, yh, x_next, :HB, :] += rb_m[r]
        xsend(r, BAUG_P, sb.at[r, yh, x_next, pl.ds(0, HB)], db_m.at[r, pl.ds(0, HB)], xp)
        xc[r, BREL_M].wait_recv()
        sb[r, yh, x_prev, HB:, :] += rb_p[r]
        xsend(r, BAUG_M, sb.at[r, yh, x_prev, pl.ds(HB, HB)], db_p.at[r, pl.ds(HB, HB)], xm)

    mc = {}

    def send_mass():
        for j in range(1, 16):
            mc[j] = send(mass.at[p], mass.at[p], ms.at[j], mr.at[j], ((p + j) % 16, z, l))
        mc[0] = send(lt.at[l], lt.at[l], ls, lr, other)

    masses = []

    def receive_mass():
        for j in range(1, 16):
            mc[j].wait_recv()
        total = mass[0]
        for j in range(1, 16):
            total += mass[j]
        masses.append(total)
        mc[0].wait_recv()
        b_ref[...] = (lt[0] + lt[1]) / 8.0 - math.log(4096)

    def finish(r):
        total = masses[0]
        row = [total[r * 4 + i : r * 4 + i + 1, :] + prior_weight for i in range(4)]
        weight = (jnp.concatenate(row[:2], axis=1), jnp.concatenate(row[2:], axis=1))
        for i in (Y_A, BPLA_P, BPLA_M, BAUG_P, BAUG_M):
            xc[r, i].wait_recv()
        high = sa[r, x, yh] + ya[r]
        low = sb[r, yh, x] + db_m[r] + db_p[r]
        moved = jnp.concatenate([high, low], axis=0).T
        for i in range(2):
            u_ref[r, :, i * HALF : (i + 1) * HALF] = (moved[i * 64 : i * 64 + 64] / weight[i]).astype(
                jnp.bfloat16
            )

    logits(0)
    pl.semaphore_wait(barrier, 23)
    send_stats(0)
    for r in range(1, REPS):
        logits(r)
        send_stats(r)
    loads[1].wait()
    steps = [(r, g) for r in range(REPS) for g in range(4)]
    stages = {"aug_a": aug_a, "rel_b": rel_b, "y_a": y_a, "aug_b": aug_b, "finish": finish}
    for i in range(len(steps) + LAG):
        late = steps[i - LAG] if i >= LAG else None
        if i < len(steps):
            r, g = steps[i]
            if g == 0:
                scale(r)
                for k in range(4):
                    weights(r, k)
            moments(r, g)
            send_moments(r, g)
        if late:
            cc[late].wait_recv()
            sum_cores(*late)
        if late:
            send_cores(*late)
        if i == 12:
            send_mass()
        for name, r in EARLY.get(i, ()):
            stages[name](r)
    receive_mass()
    for name, r in LATE:
        stages[name](r)
    for copy in sent:
        copy.wait_send()


def shards(points, centroids, counts):
    dma = pltpu.SemaphoreType.DMA
    packed, bagged = pl.pallas_call(
        kernel,
        out_shape=(
            pltpu.VMEM((REPS, 64, NK), jnp.bfloat16),
            pltpu.VMEM((1, N), F32),
        ),
        in_specs=[pl.BlockSpec(memory_space=pl.ANY)] * 3,
        out_specs=[pl.BlockSpec(memory_space=pltpu.VMEM)] * 2,
        scratch_shapes=[
            pltpu.VMEM((N, D), jnp.bfloat16),
            pltpu.VMEM((REPS, NK, D), jnp.bfloat16),
            pltpu.VMEM((REPS, N), jnp.int32),
            pltpu.VMEM((REPS, NK, N), F32),
            pltpu.VMEM((2, NK, N), jnp.bfloat16),
            pltpu.VMEM((NK, 128), F32),
            pltpu.VMEM((REPS, 1, N), F32),
            pltpu.VMEM((REPS, 8, 2, N), F32),
            pltpu.VMEM((REPS, 2, 4, 2, HALF, 128), F32),
            pltpu.VMEM((REPS, 4, 2, HALF, 128), F32),
            pltpu.VMEM((REPS, 4, 2, RA, 128), F32),
            pltpu.VMEM((REPS, 2, 4, RB, 128), F32),
            pltpu.VMEM((REPS, RA, 128), F32),
            pltpu.VMEM((REPS, RA, 128), F32),
            pltpu.VMEM((REPS, 2, RA, 128), F32),
            pltpu.VMEM((REPS, 2, RA, 128), F32),
            pltpu.VMEM((REPS, RA, 128), F32),
            pltpu.VMEM((REPS, 4, RB, 128), F32),
            pltpu.VMEM((REPS, HB, 128), F32),
            pltpu.VMEM((REPS, HB, 128), F32),
            pltpu.VMEM((REPS, RB, 128), F32),
            pltpu.VMEM((REPS, RB, 128), F32),
            pltpu.VMEM((16, 4 * REPS, 128), F32),
            pltpu.VMEM((2, 1, N), F32),
            dma((2 + REPS,)),
            dma((REPS, 8)),
            dma((REPS, 8)),
            dma((REPS, 4)),
            dma((REPS, 4)),
            dma((REPS, EXCHANGES)),
            dma((REPS, EXCHANGES)),
            dma((16,)),
            dma((16,)),
            dma,
            dma,
        ],
        compiler_params=pltpu.CompilerParams(
            collective_id=0, has_side_effects=True, vmem_limit_bytes=56 * 1024 * 1024
        ),
    )(points, centroids, counts)
    return packed.transpose(0, 2, 1), bagged.reshape(N)


def solution(mesh):
    return jax.shard_map(
        shards,
        mesh=mesh,
        in_specs=(P("dp", None), P("rep", "cent", None), P("rep", "dp")),
        out_specs=(P("rep", "cent", "dp"), P("dp")),
        check_vma=False,
    )
```

```python
import math

import jax
import jax.numpy as jnp
from jax import lax
from jax.experimental import pallas as pl
from jax.experimental.pallas import tpu as pltpu
from jax.sharding import PartitionSpec as P

MESH = pl.DeviceIdType.MESH
F32 = jnp.float32
REPS = 4
NK = 512
HALF = 256
D = 1024
N = 1024
RA = 144
RB = HALF - RA
HB = RB // 2
NT = 256
LAG = 3
OFFS = (2, 1, 3, 0)
prior_weight = 1.0

REL_P, REL_M, PLA_P, PLA_M, AUG_P, AUG_M, Y_A, BREL_P, BREL_M, BPLA_P, BPLA_M, BAUG_P, BAUG_M, Y_B = range(14)
EXCHANGES = Y_B + 4

EARLY = {9: [("aug_a", 0)], 13: [("aug_a", 1)]}
LATE = [
    ("rel_b", 0), ("aug_a", 2), ("mass_y", 0), ("y_a", 0), ("rel_b", 1), ("aug_a", 3), ("aug_b", 0), ("y_a", 1), ("rel_b", 2),
    ("aug_b", 1), ("y_a", 2), ("rel_b", 3), ("aug_b", 2), ("y_a", 3), ("mass", 0), ("finish", 0), ("finish", 1),
    ("aug_b", 3), ("finish", 2), ("finish", 3),
]


def pack(top, low):
    first = lax.broadcasted_iota(jnp.int32, top.shape, 1) < 64
    swapped = pltpu.roll(jnp.where(first, low, top), 64, 1)
    return jnp.where(first, top, swapped), jnp.where(first, swapped, low)


def kernel(
    p_hbm, c_hbm, n_hbm, u_ref, b_ref,
    p_v, c_v, n_v, e_v, w_v, hs_v, sc_v, st, mp, cr, sa, sb,
    ra_m, ra_p, da_m, da_p, ya, yb, rb_m, rb_p, db_m, db_p, mass, lt,
    ld, zs, zr, cs, crs, xs, xr, ms, mr, ls, lr,
):
    p = lax.axis_index("dp")
    z = lax.axis_index("cent")
    l = lax.axis_index("rep")
    c = p % 2
    x = (p // 2) % 4
    yh = p // 8
    sib = (p + 1 - 2 * c, z, l)
    xp = (yh * 8 + ((x + 1) % 4) * 2 + c, z, l)
    xm = (yh * 8 + ((x + 3) % 4) * 2 + c, z, l)
    x2 = (yh * 8 + ((x + 2) % 4) * 2 + c, z, l)
    y2 = ((1 - yh) * 8 + x * 2 + c, z, l)
    other = (p, z, 1 - l)

    loads = [pltpu.make_async_copy(p_hbm, p_v, ld.at[0])]
    loads.append(pltpu.make_async_copy(n_hbm, n_v, ld.at[1]))
    for r in range(REPS):
        loads.append(pltpu.make_async_copy(c_hbm.at[r], c_v.at[r], ld.at[2 + r]))
    for i in (2, 0, 3, 4, 5, 1):
        loads[i].start()

    barrier = pltpu.get_barrier_semaphore()
    peers = [(p, (z + j) % 8, l) for j in (4, 3, 5, 2, 6, 1, 7)] + [x2, y2, xp, xm, sib, other]
    for peer in peers:
        pl.semaphore_signal(barrier, inc=1, device_id=peer, device_id_type=MESH)

    sent = []

    def send(src, dst, ssem, rsem, dev):
        copy = pltpu.make_async_remote_copy(
            src_ref=src, dst_ref=dst, send_sem=ssem, recv_sem=rsem, device_id=dev, device_id_type=MESH
        )
        copy.start()
        sent.append(copy)
        return copy

    def logits(r):
        loads[2 + r].wait()
        if r == 0:
            loads[0].wait()
        for i in range(0, NK, 64):
            block = c_v[r, i : i + 64, :].astype(F32)
            hs_v[i : i + 64, :] = jnp.broadcast_to(
                0.5 * jnp.sum(block * block, axis=1, keepdims=True), (64, 128)
            )

        for t in range(0, N, NT):
            cols = slice(t, t + NT)
            half = hs_v[...]
            tile = lax.dot_general(
                c_v[r], p_v[cols, :], (((1,), (1,)), ((), ())), preferred_element_type=F32
            ) - jnp.concatenate([half, half], axis=1)
            top = jnp.max(tile, axis=0, keepdims=True)
            tile = jnp.exp(tile - top)
            e_v[r, :, cols] = tile
            st[r, z, 0:1, cols] = top
            st[r, z, 1:2, cols] = jnp.sum(tile, axis=0, keepdims=True)

    zc = {}

    def send_stats(r):
        for j in range(1, 8):
            zc[r, j] = send(st.at[r, z], st.at[r, z], zs.at[r, j], zr.at[r, j], (p, (z + j) % 8, l))

    cc = {}

    def scale(r):
        for j in range(1, 8):
            zc[r, j].wait_recv()
        top = st[r, 0, 0:1, :]
        for j in range(1, 8):
            top = jnp.maximum(top, st[r, j, 0:1, :])
        total = jnp.zeros_like(top)
        for j in range(8):
            total += st[r, j, 1:2, :] * jnp.exp(st[r, j, 0:1, :] - top)
        sc_v[r, :, :] = jnp.exp(st[r, z, 0:1, :] - top) / total * n_v[r : r + 1, :].astype(F32)
        log_total = top + jnp.log(total)
        if r == 0:
            lt[l, :, :] = log_total
        else:
            lt[l, :, :] += log_total

    def weights(r, g):
        factor = sc_v[r]
        parts = []
        for i in range(g * 128, g * 128 + 128, 32):
            w = (e_v[r, i : i + 32, :] * factor).astype(jnp.bfloat16)
            w_v[r % 2, i : i + 32, :] = w
            w = w.astype(F32)
            part = w[:, :128]
            for k in range(128, N, 128):
                part = part + w[:, k : k + 128]
            parts.append(part)
        part = jnp.concatenate(parts, axis=0).T
        mass[0, r * 4 + g : r * 4 + g + 1, :] = jnp.sum(part, axis=0, keepdims=True)

    def moments(r, g):
        xx = (x + OFFS[g]) % 4
        lo = pl.ds(pl.multiple_of(xx * 128, 128), 128)
        hi = pl.ds(pl.multiple_of(512 + xx * 128, 128), 128)
        block = jnp.concatenate([p_v[:, lo], p_v[:, hi]], axis=1)
        out = jnp.dot(w_v[r % 2], block, preferred_element_type=F32)
        for h in range(2):
            part = out[:, h * 128 : (h + 1) * 128]
            zero, one = pack(part[:HALF], part[HALF:])
            mp[r, 0, xx, h, :, :] = zero
            mp[r, 1, xx, h, :, :] = one

    cc = {}

    def send_moments(r, g):
        xx = (x + OFFS[g]) % 4
        cc[r, g] = send(mp.at[r, 1 - c, xx], cr.at[r, xx], cs.at[r, g], crs.at[r, g], sib)

    xc = {}

    def xsend(r, i, src, dst, dev):
        xc[r, i] = send(src, dst, xs.at[r, i], xr.at[r, i], dev)

    x_opp, x_next, x_prev = (x + 2) % 4, (x + 1) % 4, (x + 3) % 4

    def own_centroids(r):
        q = pl.ds(pl.multiple_of((yh * 4 + x) * 128, 128), 128)
        zero, one = pack(c_v[r, :HALF, q].astype(F32), c_v[r, HALF:, q].astype(F32))
        return prior_weight * jnp.where(jnp.full((HALF, 128), c, jnp.int32) == 0, zero, one)

    def sum_cores(r, g):
        xx = (x + OFFS[g]) % 4
        for h in range(2):
            sa[r, xx, h, :, :] = mp[r, c, xx, h, :RA, :] + cr[r, xx, h, :RA, :]
            sb[r, h, xx, :, :] = mp[r, c, xx, h, RA:, :] + cr[r, xx, h, RA:, :]
        if g == 3:
            own = own_centroids(r)
            sa[r, x, yh, :, :] += own[:RA]
            sb[r, yh, x, :, :] += own[RA:]

    def send_cores(r, g):
        if g == 0:
            xsend(r, REL_P, sa.at[r, x_opp, 0], ra_m.at[r], xp)
            xsend(r, REL_M, sa.at[r, x_opp, 1], ra_p.at[r], xm)
        if g == 1:
            xsend(r, PLA_P, sa.at[r, x_next, 1], da_m.at[r, 1], xp)
        if g == 2:
            xsend(r, PLA_M, sa.at[r, x_prev, 0], da_p.at[r, 0], xm)
        xx = (x + OFFS[g]) % 4
        xsend(r, Y_B + g, sb.at[r, 1 - yh, xx], yb.at[r, xx], y2)

    def aug_a(r):
        xc[r, REL_P].wait_recv()
        sa[r, x_next, 0, :, :] += ra_m[r]
        xsend(r, AUG_P, sa.at[r, x_next, 0], da_m.at[r, 0], xp)
        xc[r, REL_M].wait_recv()
        sa[r, x_prev, 1, :, :] += ra_p[r]
        xsend(r, AUG_M, sa.at[r, x_prev, 1], da_p.at[r, 1], xm)

    def rel_b(r):
        xc[r, Y_B].wait_recv()
        sb[r, yh, x_opp, :, :] += yb[r, x_opp]
        xsend(r, BREL_P, sb.at[r, yh, x_opp, pl.ds(0, HB)], rb_m.at[r], xp)
        xsend(r, BREL_M, sb.at[r, yh, x_opp, pl.ds(HB, HB)], rb_p.at[r], xm)
        xc[r, Y_B + 1].wait_recv()
        sb[r, yh, x_next, :, :] += yb[r, x_next]
        xsend(r, BPLA_P, sb.at[r, yh, x_next, pl.ds(HB, HB)], db_m.at[r, pl.ds(HB, HB)], xp)
        xc[r, Y_B + 2].wait_recv()
        sb[r, yh, x_prev, :, :] += yb[r, x_prev]
        xsend(r, BPLA_M, sb.at[r, yh, x_prev, pl.ds(0, HB)], db_p.at[r, pl.ds(0, HB)], xm)
        xc[r, Y_B + 3].wait_recv()
        sb[r, yh, x, :, :] += yb[r, x]

    def y_a(r):
        for i in (PLA_P, PLA_M, AUG_P, AUG_M):
            xc[r, i].wait_recv()
        sa[r, x, 1 - yh, :, :] += da_m[r, 1 - yh] + da_p[r, 1 - yh]
        xsend(r, Y_A, sa.at[r, x, 1 - yh], ya.at[r], y2)
        sa[r, x, yh, :, :] += da_m[r, yh] + da_p[r, yh]

    def aug_b(r):
        xc[r, BREL_P].wait_recv()
        sb[r, yh, x_next, :HB, :] += rb_m[r]
        xsend(r, BAUG_P, sb.at[r, yh, x_next, pl.ds(0, HB)], db_m.at[r, pl.ds(0, HB)], xp)
        xc[r, BREL_M].wait_recv()
        sb[r, yh, x_prev, HB:, :] += rb_p[r]
        xsend(r, BAUG_M, sb.at[r, yh, x_prev, pl.ds(HB, HB)], db_p.at[r, pl.ds(HB, HB)], xm)

    mc = {}

    def mass_send(i, src, dst, dev):
        mc[i] = send(mass.at[src], mass.at[dst], ms.at[i], mr.at[i], dev)

    def mass_core():
        mass_send(0, 0, 1, sib)
        mc["lt"] = send(lt.at[l], lt.at[l], ls, lr, other)

    def mass_x():
        mc[0].wait_recv()
        mass[2, :, :] = mass[0] + mass[1]
        for j, dev in ((1, xp), (2, x2), (3, xm)):
            mass_send(j, 2, 2 + j, dev)

    def mass_y():
        for j in (1, 2, 3):
            mc[j].wait_recv()
        mass[6, :, :] = mass[2] + mass[3] + mass[4] + mass[5]
        mass_send(4, 6, 7, y2)

    masses = []

    def receive_mass():
        mc[4].wait_recv()
        masses.append(mass[6] + mass[7])
        mc["lt"].wait_recv()
        b_ref[...] = (lt[0] + lt[1]) / 8.0 - math.log(4096)

    def finish(r):
        total = masses[0]
        row = [total[r * 4 + i : r * 4 + i + 1, :] + prior_weight for i in range(4)]
        weight = (jnp.concatenate(row[:2], axis=1), jnp.concatenate(row[2:], axis=1))
        for i in (Y_A, BPLA_P, BPLA_M, BAUG_P, BAUG_M):
            xc[r, i].wait_recv()
        high = sa[r, x, yh] + ya[r]
        low = sb[r, yh, x] + db_m[r] + db_p[r]
        moved = jnp.concatenate([high, low], axis=0).T
        for i in range(2):
            u_ref[r, :, i * HALF : (i + 1) * HALF] = (moved[i * 64 : i * 64 + 64] / weight[i]).astype(
                jnp.bfloat16
            )

    logits(0)
    pl.semaphore_wait(barrier, len(peers))
    send_stats(0)
    for r in range(1, REPS):
        logits(r)
        send_stats(r)
    loads[1].wait()
    steps = [(r, g) for r in range(REPS) for g in range(4)]
    stages = {"aug_a": aug_a, "rel_b": rel_b, "y_a": y_a, "aug_b": aug_b, "finish": finish}
    for i in range(len(steps) + LAG):
        late = steps[i - LAG] if i >= LAG else None
        if i < len(steps):
            r, g = steps[i]
            if g == 0:
                scale(r)
                for k in range(4):
                    weights(r, k)
            moments(r, g)
            send_moments(r, g)
        if late:
            cc[late].wait_recv()
            sum_cores(*late)
        if late:
            send_cores(*late)
        if i == 12:
            mass_core()
        if i == 15:
            mass_x()
        for name, r in EARLY.get(i, ()):
            stages[name](r)
    for name, r in LATE:
        if name == "mass_y":
            mass_y()
        elif name == "mass":
            receive_mass()
        else:
            stages[name](r)
    for copy in sent:
        copy.wait_send()


def shards(points, centroids, counts):
    dma = pltpu.SemaphoreType.DMA
    packed, bagged = pl.pallas_call(
        kernel,
        out_shape=(
            pltpu.VMEM((REPS, 64, NK), jnp.bfloat16),
            pltpu.VMEM((1, N), F32),
        ),
        in_specs=[pl.BlockSpec(memory_space=pl.ANY)] * 3,
        out_specs=[pl.BlockSpec(memory_space=pltpu.VMEM)] * 2,
        scratch_shapes=[
            pltpu.VMEM((N, D), jnp.bfloat16),
            pltpu.VMEM((REPS, NK, D), jnp.bfloat16),
            pltpu.VMEM((REPS, N), jnp.int32),
            pltpu.VMEM((REPS, NK, N), F32),
            pltpu.VMEM((2, NK, N), jnp.bfloat16),
            pltpu.VMEM((NK, 128), F32),
            pltpu.VMEM((REPS, 1, N), F32),
            pltpu.VMEM((REPS, 8, 2, N), F32),
            pltpu.VMEM((REPS, 2, 4, 2, HALF, 128), F32),
            pltpu.VMEM((REPS, 4, 2, HALF, 128), F32),
            pltpu.VMEM((REPS, 4, 2, RA, 128), F32),
            pltpu.VMEM((REPS, 2, 4, RB, 128), F32),
            pltpu.VMEM((REPS, RA, 128), F32),
            pltpu.VMEM((REPS, RA, 128), F32),
            pltpu.VMEM((REPS, 2, RA, 128), F32),
            pltpu.VMEM((REPS, 2, RA, 128), F32),
            pltpu.VMEM((REPS, RA, 128), F32),
            pltpu.VMEM((REPS, 4, RB, 128), F32),
            pltpu.VMEM((REPS, HB, 128), F32),
            pltpu.VMEM((REPS, HB, 128), F32),
            pltpu.VMEM((REPS, RB, 128), F32),
            pltpu.VMEM((REPS, RB, 128), F32),
            pltpu.VMEM((8, 4 * REPS, 128), F32),
            pltpu.VMEM((2, 1, N), F32),
            dma((2 + REPS,)),
            dma((REPS, 8)),
            dma((REPS, 8)),
            dma((REPS, 4)),
            dma((REPS, 4)),
            dma((REPS, EXCHANGES)),
            dma((REPS, EXCHANGES)),
            dma((5,)),
            dma((5,)),
            dma,
            dma,
        ],
        compiler_params=pltpu.CompilerParams(
            collective_id=0, has_side_effects=True, vmem_limit_bytes=56 * 1024 * 1024
        ),
    )(points, centroids, counts)
    return packed.transpose(0, 2, 1), bagged.reshape(N)


def solution(mesh):
    return jax.shard_map(
        shards,
        mesh=mesh,
        in_specs=(P("dp", None), P("rep", "cent", None), P("rep", "dp")),
        out_specs=(P("rep", "cent", "dp"), P("dp")),
        check_vma=False,
    )
```

```python
import math

import jax
import jax.numpy as jnp
from jax import lax
from jax.experimental import pallas as pl
from jax.experimental.pallas import tpu as pltpu
from jax.sharding import PartitionSpec as P

MESH = pl.DeviceIdType.MESH
F32 = jnp.float32
REPS = 4
NK = 512
HALF = 256
D = 1024
N = 1024
RA = 144
RB = HALF - RA
HB = RB // 2
NT = 256
LAG = 2
OFFS = (2, 1, 3, 0)
prior_weight = 1.0

REL_P, REL_M, PLA_P, PLA_M, AUG_P, AUG_M, Y_A, BREL_P, BREL_M, BPLA_P, BPLA_M, BAUG_P, BAUG_M, Y_B = range(14)
EXCHANGES = Y_B + 4

EARLY = {9: [("aug_a", 0)], 13: [("aug_a", 1)]}
LATE = [
    ("aug_a", 2), ("rel_b", 0), ("mass_y", 0), ("y_a", 0), ("aug_a", 3), ("rel_b", 1), ("y_a", 1), ("aug_b", 0),
    ("rel_b", 2), ("y_a", 2), ("aug_b", 1), ("rel_b", 3), ("y_a", 3), ("aug_b", 2), ("aug_b", 3), ("mass", 0),
    ("finish", 0), ("finish", 1), ("finish", 2), ("finish", 3),
]


def pack(top, low):
    first = lax.broadcasted_iota(jnp.int32, top.shape, 1) < 64
    swapped = pltpu.roll(jnp.where(first, low, top), 64, 1)
    return jnp.where(first, top, swapped), jnp.where(first, swapped, low)


def kernel(
    p_hbm, c_hbm, n_hbm, u_ref, b_ref,
    p_v, c_v, n_v, e_v, w_v, hs_v, sc_v, st, mp, cr, sa, sb,
    ra_m, ra_p, da_m, da_p, ya, yb, rb_m, rb_p, db_m, db_p, mass, lt,
    ld, zs, zr, cs, crs, xs, xr, ms, mr, ls, lr,
):
    p = lax.axis_index("dp")
    z = lax.axis_index("cent")
    l = lax.axis_index("rep")
    c = p % 2
    x = (p // 2) % 4
    yh = p // 8
    sib = (p + 1 - 2 * c, z, l)
    xp = (yh * 8 + ((x + 1) % 4) * 2 + c, z, l)
    xm = (yh * 8 + ((x + 3) % 4) * 2 + c, z, l)
    x2 = (yh * 8 + ((x + 2) % 4) * 2 + c, z, l)
    y2 = ((1 - yh) * 8 + x * 2 + c, z, l)
    other = (p, z, 1 - l)

    loads = [pltpu.make_async_copy(p_hbm, p_v, ld.at[0])]
    loads.append(pltpu.make_async_copy(n_hbm, n_v, ld.at[1]))
    for r in range(REPS):
        loads.append(pltpu.make_async_copy(c_hbm.at[r], c_v.at[r], ld.at[2 + r]))
    for i in (2, 0, 3, 4, 5, 1):
        loads[i].start()

    barrier = pltpu.get_barrier_semaphore()
    peers = [(p, (z + j) % 8, l) for j in (4, 3, 5, 2, 6, 1, 7)] + [x2, y2, xp, xm, sib, other]
    for peer in peers:
        pl.semaphore_signal(barrier, inc=1, device_id=peer, device_id_type=MESH)

    sent = []

    def send(src, dst, ssem, rsem, dev):
        copy = pltpu.make_async_remote_copy(
            src_ref=src, dst_ref=dst, send_sem=ssem, recv_sem=rsem, device_id=dev, device_id_type=MESH
        )
        copy.start()
        sent.append(copy)
        return copy

    def logits(r):
        loads[2 + r].wait()
        if r == 0:
            loads[0].wait()
        for i in range(0, NK, 64):
            block = c_v[r, i : i + 64, :].astype(F32)
            hs_v[i : i + 64, :] = jnp.broadcast_to(
                0.5 * jnp.sum(block * block, axis=1, keepdims=True), (64, 128)
            )

        for t in range(0, N, NT):
            cols = slice(t, t + NT)
            half = hs_v[...]
            tile = lax.dot_general(
                c_v[r], p_v[cols, :], (((1,), (1,)), ((), ())), preferred_element_type=F32
            ) - jnp.concatenate([half, half], axis=1)
            top = jnp.max(tile, axis=0, keepdims=True)
            tile = jnp.exp(tile - top)
            e_v[r, :, cols] = tile
            st[r, z, 0:1, cols] = top
            st[r, z, 1:2, cols] = jnp.sum(tile, axis=0, keepdims=True)

    zc = {}

    def send_stats(r):
        for j in range(1, 8):
            zc[r, j] = send(st.at[r, z], st.at[r, z], zs.at[r, j], zr.at[r, j], (p, (z + j) % 8, l))

    cc = {}

    def scale(r):
        for j in range(1, 8):
            zc[r, j].wait_recv()
        top = st[r, 0, 0:1, :]
        for j in range(1, 8):
            top = jnp.maximum(top, st[r, j, 0:1, :])
        total = jnp.zeros_like(top)
        for j in range(8):
            total += st[r, j, 1:2, :] * jnp.exp(st[r, j, 0:1, :] - top)
        sc_v[r, :, :] = jnp.exp(st[r, z, 0:1, :] - top) / total * n_v[r : r + 1, :].astype(F32)
        log_total = top + jnp.log(total)
        if r == 0:
            lt[l, :, :] = log_total
        else:
            lt[l, :, :] += log_total

    def weights(r, g):
        factor = sc_v[r]
        parts = []
        for i in range(g * 128, g * 128 + 128, 32):
            w = (e_v[r, i : i + 32, :] * factor).astype(jnp.bfloat16)
            w_v[r % 2, i : i + 32, :] = w
            w = w.astype(F32)
            part = w[:, :128]
            for k in range(128, N, 128):
                part = part + w[:, k : k + 128]
            parts.append(part)
        part = jnp.concatenate(parts, axis=0).T
        mass[0, r * 4 + g : r * 4 + g + 1, :] = jnp.sum(part, axis=0, keepdims=True)

    def moments(r, g):
        xx = (x + OFFS[g]) % 4
        lo = pl.ds(pl.multiple_of(xx * 128, 128), 128)
        hi = pl.ds(pl.multiple_of(512 + xx * 128, 128), 128)
        block = jnp.concatenate([p_v[:, lo], p_v[:, hi]], axis=1)
        out = jnp.dot(w_v[r % 2], block, preferred_element_type=F32)
        for h in range(2):
            part = out[:, h * 128 : (h + 1) * 128]
            zero, one = pack(part[:HALF], part[HALF:])
            mp[r, 0, xx, h, :, :] = zero
            mp[r, 1, xx, h, :, :] = one

    cc = {}

    def send_moments(r, g):
        xx = (x + OFFS[g]) % 4
        cc[r, g] = send(mp.at[r, 1 - c, xx], cr.at[r, xx], cs.at[r, g], crs.at[r, g], sib)

    xc = {}

    def xsend(r, i, src, dst, dev):
        xc[r, i] = send(src, dst, xs.at[r, i], xr.at[r, i], dev)

    x_opp, x_next, x_prev = (x + 2) % 4, (x + 1) % 4, (x + 3) % 4

    def own_centroids(r):
        q = pl.ds(pl.multiple_of((yh * 4 + x) * 128, 128), 128)
        zero, one = pack(c_v[r, :HALF, q].astype(F32), c_v[r, HALF:, q].astype(F32))
        return prior_weight * jnp.where(jnp.full((HALF, 128), c, jnp.int32) == 0, zero, one)

    def sum_cores(r, g):
        xx = (x + OFFS[g]) % 4
        for h in range(2):
            sa[r, xx, h, :, :] = mp[r, c, xx, h, :RA, :] + cr[r, xx, h, :RA, :]
            sb[r, h, xx, :, :] = mp[r, c, xx, h, RA:, :] + cr[r, xx, h, RA:, :]
        if g == 3:
            own = own_centroids(r)
            sa[r, x, yh, :, :] += own[:RA]
            sb[r, yh, x, :, :] += own[RA:]

    def send_cores(r, g):
        if g == 0:
            xsend(r, REL_P, sa.at[r, x_opp, 0], ra_m.at[r], xp)
            xsend(r, REL_M, sa.at[r, x_opp, 1], ra_p.at[r], xm)
        if g == 1:
            xsend(r, PLA_P, sa.at[r, x_next, 1], da_m.at[r, 1], xp)
        if g == 2:
            xsend(r, PLA_M, sa.at[r, x_prev, 0], da_p.at[r, 0], xm)
        xx = (x + OFFS[g]) % 4
        xsend(r, Y_B + g, sb.at[r, 1 - yh, xx], yb.at[r, xx], y2)

    def aug_a(r):
        xc[r, REL_P].wait_recv()
        sa[r, x_next, 0, :, :] += ra_m[r]
        xsend(r, AUG_P, sa.at[r, x_next, 0], da_m.at[r, 0], xp)
        xc[r, REL_M].wait_recv()
        sa[r, x_prev, 1, :, :] += ra_p[r]
        xsend(r, AUG_M, sa.at[r, x_prev, 1], da_p.at[r, 1], xm)

    def rel_b(r):
        xc[r, Y_B].wait_recv()
        sb[r, yh, x_opp, :, :] += yb[r, x_opp]
        xsend(r, BREL_P, sb.at[r, yh, x_opp, pl.ds(0, HB)], rb_m.at[r], xp)
        xsend(r, BREL_M, sb.at[r, yh, x_opp, pl.ds(HB, HB)], rb_p.at[r], xm)
        xc[r, Y_B + 1].wait_recv()
        sb[r, yh, x_next, :, :] += yb[r, x_next]
        xsend(r, BPLA_P, sb.at[r, yh, x_next, pl.ds(HB, HB)], db_m.at[r, pl.ds(HB, HB)], xp)
        xc[r, Y_B + 2].wait_recv()
        sb[r, yh, x_prev, :, :] += yb[r, x_prev]
        xsend(r, BPLA_M, sb.at[r, yh, x_prev, pl.ds(0, HB)], db_p.at[r, pl.ds(0, HB)], xm)
        xc[r, Y_B + 3].wait_recv()
        sb[r, yh, x, :, :] += yb[r, x]

    def y_a(r):
        for i in (PLA_P, PLA_M, AUG_P, AUG_M):
            xc[r, i].wait_recv()
        sa[r, x, 1 - yh, :, :] += da_m[r, 1 - yh] + da_p[r, 1 - yh]
        xsend(r, Y_A, sa.at[r, x, 1 - yh], ya.at[r], y2)
        sa[r, x, yh, :, :] += da_m[r, yh] + da_p[r, yh]

    def aug_b(r):
        xc[r, BREL_P].wait_recv()
        sb[r, yh, x_next, :HB, :] += rb_m[r]
        xsend(r, BAUG_P, sb.at[r, yh, x_next, pl.ds(0, HB)], db_m.at[r, pl.ds(0, HB)], xp)
        xc[r, BREL_M].wait_recv()
        sb[r, yh, x_prev, HB:, :] += rb_p[r]
        xsend(r, BAUG_M, sb.at[r, yh, x_prev, pl.ds(HB, HB)], db_p.at[r, pl.ds(HB, HB)], xm)

    mc = {}

    def mass_send(i, src, dst, dev):
        mc[i] = send(mass.at[src], mass.at[dst], ms.at[i], mr.at[i], dev)

    def mass_core():
        mass_send(0, 0, 1, sib)
        mc["lt"] = send(lt.at[l], lt.at[l], ls, lr, other)

    def mass_x():
        mc[0].wait_recv()
        mass[2, :, :] = mass[0] + mass[1]
        for j, dev in ((1, xp), (2, x2), (3, xm)):
            mass_send(j, 2, 2 + j, dev)

    def mass_y():
        for j in (1, 2, 3):
            mc[j].wait_recv()
        mass[6, :, :] = mass[2] + mass[3] + mass[4] + mass[5]
        mass_send(4, 6, 7, y2)

    masses = []

    def receive_mass():
        mc[4].wait_recv()
        masses.append(mass[6] + mass[7])
        mc["lt"].wait_recv()
        b_ref[...] = (lt[0] + lt[1]) / 8.0 - math.log(4096)

    def finish(r):
        total = masses[0]
        row = [total[r * 4 + i : r * 4 + i + 1, :] + prior_weight for i in range(4)]
        weight = (jnp.concatenate(row[:2], axis=1), jnp.concatenate(row[2:], axis=1))
        for i in (Y_A, BPLA_P, BPLA_M, BAUG_P, BAUG_M):
            xc[r, i].wait_recv()
        high = sa[r, x, yh] + ya[r]
        low = sb[r, yh, x] + db_m[r] + db_p[r]
        moved = jnp.concatenate([high, low], axis=0).T
        for i in range(2):
            u_ref[r, :, i * HALF : (i + 1) * HALF] = (moved[i * 64 : i * 64 + 64] / weight[i]).astype(
                jnp.bfloat16
            )

    logits(0)
    pl.semaphore_wait(barrier, len(peers))
    send_stats(0)
    for r in range(1, REPS):
        logits(r)
        send_stats(r)
    loads[1].wait()
    steps = [(r, g) for r in range(REPS) for g in range(4)]
    stages = {"aug_a": aug_a, "rel_b": rel_b, "y_a": y_a, "aug_b": aug_b, "finish": finish}
    for i in range(len(steps) + LAG):
        late = steps[i - LAG] if i >= LAG else None
        if i < len(steps):
            r, g = steps[i]
            if g == 0:
                scale(r)
                for k in range(4):
                    weights(r, k)
            moments(r, g)
            send_moments(r, g)
        if late:
            cc[late].wait_recv()
            sum_cores(*late)
        if late:
            send_cores(*late)
        if i == 12:
            mass_core()
        if i == 15:
            mass_x()
        for name, r in EARLY.get(i, ()):
            stages[name](r)
    for name, r in LATE:
        if name == "mass_y":
            mass_y()
        elif name == "mass":
            receive_mass()
        else:
            stages[name](r)
    for copy in sent:
        copy.wait_send()


def shards(points, centroids, counts):
    dma = pltpu.SemaphoreType.DMA
    packed, bagged = pl.pallas_call(
        kernel,
        out_shape=(
            pltpu.VMEM((REPS, 64, NK), jnp.bfloat16),
            pltpu.VMEM((1, N), F32),
        ),
        in_specs=[pl.BlockSpec(memory_space=pl.ANY)] * 3,
        out_specs=[pl.BlockSpec(memory_space=pltpu.VMEM)] * 2,
        scratch_shapes=[
            pltpu.VMEM((N, D), jnp.bfloat16),
            pltpu.VMEM((REPS, NK, D), jnp.bfloat16),
            pltpu.VMEM((REPS, N), jnp.int32),
            pltpu.VMEM((REPS, NK, N), F32),
            pltpu.VMEM((2, NK, N), jnp.bfloat16),
            pltpu.VMEM((NK, 128), F32),
            pltpu.VMEM((REPS, 1, N), F32),
            pltpu.VMEM((REPS, 8, 2, N), F32),
            pltpu.VMEM((REPS, 2, 4, 2, HALF, 128), F32),
            pltpu.VMEM((REPS, 4, 2, HALF, 128), F32),
            pltpu.VMEM((REPS, 4, 2, RA, 128), F32),
            pltpu.VMEM((REPS, 2, 4, RB, 128), F32),
            pltpu.VMEM((REPS, RA, 128), F32),
            pltpu.VMEM((REPS, RA, 128), F32),
            pltpu.VMEM((REPS, 2, RA, 128), F32),
            pltpu.VMEM((REPS, 2, RA, 128), F32),
            pltpu.VMEM((REPS, RA, 128), F32),
            pltpu.VMEM((REPS, 4, RB, 128), F32),
            pltpu.VMEM((REPS, HB, 128), F32),
            pltpu.VMEM((REPS, HB, 128), F32),
            pltpu.VMEM((REPS, RB, 128), F32),
            pltpu.VMEM((REPS, RB, 128), F32),
            pltpu.VMEM((8, 4 * REPS, 128), F32),
            pltpu.VMEM((2, 1, N), F32),
            dma((2 + REPS,)),
            dma((REPS, 8)),
            dma((REPS, 8)),
            dma((REPS, 4)),
            dma((REPS, 4)),
            dma((REPS, EXCHANGES)),
            dma((REPS, EXCHANGES)),
            dma((5,)),
            dma((5,)),
            dma,
            dma,
        ],
        compiler_params=pltpu.CompilerParams(
            collective_id=0, has_side_effects=True, vmem_limit_bytes=56 * 1024 * 1024
        ),
    )(points, centroids, counts)
    return packed.transpose(0, 2, 1), bagged.reshape(N)


def solution(mesh):
    return jax.shard_map(
        shards,
        mesh=mesh,
        in_specs=(P("dp", None), P("rep", "cent", None), P("rep", "dp")),
        out_specs=(P("rep", "cent", "dp"), P("dp")),
        check_vma=False,
    )
```

```python
import math

import jax
import jax.numpy as jnp
from jax import lax
from jax.experimental import pallas as pl
from jax.experimental.pallas import tpu as pltpu
from jax.sharding import PartitionSpec as P

MESH = pl.DeviceIdType.MESH
F32 = jnp.float32
REPS = 4
NK = 512
HALF = 256
D = 1024
N = 1024
SPLIT = (160, 144, 144, 128)
RA = max(SPLIT)
RB = HALF - min(SPLIT)
HB = RB // 2
NT = 256
LAG = 2
OFFS = (2, 1, 3, 0)
prior_weight = 1.0

REL_P, REL_M, PLA_P, PLA_M, AUG_P, AUG_M, Y_A, BREL_P, BREL_M, BPLA_P, BPLA_M, BAUG_P, BAUG_M, Y_B = range(14)
EXCHANGES = Y_B + 4

EARLY = {9: [("aug_a", 0)], 13: [("aug_a", 1)]}
LATE = [
    ("aug_a", 2), ("rel_b", 0), ("mass_y", 0), ("y_a", 0), ("aug_a", 3), ("rel_b", 1), ("y_a", 1), ("aug_b", 0),
    ("rel_b", 2), ("y_a", 2), ("aug_b", 1), ("rel_b", 3), ("y_a", 3), ("aug_b", 2), ("aug_b", 3), ("mass", 0),
    ("finish", 0), ("finish", 1), ("finish", 2), ("finish", 3),
]


def pack(top, low):
    first = lax.broadcasted_iota(jnp.int32, top.shape, 1) < 64
    swapped = pltpu.roll(jnp.where(first, low, top), 64, 1)
    return jnp.where(first, top, swapped), jnp.where(first, swapped, low)


def kernel(
    p_hbm, c_hbm, n_hbm, u_ref, b_ref,
    p_v, c_v, n_v, e_v, w_v, hs_v, sc_v, st, mp, cr, sa, sb,
    ra_m, ra_p, da_m, da_p, ya, yb, rb_m, rb_p, db_m, db_p, mass, lt,
    ld, zs, zr, cs, crs, xs, xr, ms, mr, ls, lr,
):
    p = lax.axis_index("dp")
    z = lax.axis_index("cent")
    l = lax.axis_index("rep")
    c = p % 2
    x = (p // 2) % 4
    yh = p // 8
    sib = (p + 1 - 2 * c, z, l)
    xp = (yh * 8 + ((x + 1) % 4) * 2 + c, z, l)
    xm = (yh * 8 + ((x + 3) % 4) * 2 + c, z, l)
    x2 = (yh * 8 + ((x + 2) % 4) * 2 + c, z, l)
    y2 = ((1 - yh) * 8 + x * 2 + c, z, l)
    other = (p, z, 1 - l)

    loads = [pltpu.make_async_copy(p_hbm, p_v, ld.at[0])]
    loads.append(pltpu.make_async_copy(n_hbm, n_v, ld.at[1]))
    for r in range(REPS):
        loads.append(pltpu.make_async_copy(c_hbm.at[r], c_v.at[r], ld.at[2 + r]))
    for i in (2, 0, 3, 4, 5, 1):
        loads[i].start()

    barrier = pltpu.get_barrier_semaphore()
    peers = [(p, (z + j) % 8, l) for j in (4, 3, 5, 2, 6, 1, 7)] + [x2, y2, xp, xm, sib, other]
    for peer in peers:
        pl.semaphore_signal(barrier, inc=1, device_id=peer, device_id_type=MESH)

    sent = []

    def send(src, dst, ssem, rsem, dev):
        copy = pltpu.make_async_remote_copy(
            src_ref=src, dst_ref=dst, send_sem=ssem, recv_sem=rsem, device_id=dev, device_id_type=MESH
        )
        copy.start()
        sent.append(copy)
        return copy

    def logits(r):
        loads[2 + r].wait()
        if r == 0:
            loads[0].wait()
        for i in range(0, NK, 64):
            block = c_v[r, i : i + 64, :].astype(F32)
            hs_v[i : i + 64, :] = jnp.broadcast_to(
                0.5 * jnp.sum(block * block, axis=1, keepdims=True), (64, 128)
            )

        for t in range(0, N, NT):
            cols = slice(t, t + NT)
            half = hs_v[...]
            tile = lax.dot_general(
                c_v[r], p_v[cols, :], (((1,), (1,)), ((), ())), preferred_element_type=F32
            ) - jnp.concatenate([half, half], axis=1)
            top = jnp.max(tile, axis=0, keepdims=True)
            tile = jnp.exp(tile - top)
            e_v[r, :, cols] = tile
            st[r, z, 0:1, cols] = top
            st[r, z, 1:2, cols] = jnp.sum(tile, axis=0, keepdims=True)

    zc = {}

    def send_stats(r):
        for j in range(1, 8):
            zc[r, j] = send(st.at[r, z], st.at[r, z], zs.at[r, j], zr.at[r, j], (p, (z + j) % 8, l))

    cc = {}

    def scale(r):
        for j in range(1, 8):
            zc[r, j].wait_recv()
        top = st[r, 0, 0:1, :]
        for j in range(1, 8):
            top = jnp.maximum(top, st[r, j, 0:1, :])
        total = jnp.zeros_like(top)
        for j in range(8):
            total += st[r, j, 1:2, :] * jnp.exp(st[r, j, 0:1, :] - top)
        sc_v[r, :, :] = jnp.exp(st[r, z, 0:1, :] - top) / total * n_v[r : r + 1, :].astype(F32)
        log_total = top + jnp.log(total)
        if r == 0:
            lt[l, :, :] = log_total
        else:
            lt[l, :, :] += log_total

    def weights(r, g):
        factor = sc_v[r]
        parts = []
        for i in range(g * 128, g * 128 + 128, 32):
            w = (e_v[r, i : i + 32, :] * factor).astype(jnp.bfloat16)
            w_v[r % 2, i : i + 32, :] = w
            w = w.astype(F32)
            part = w[:, :128]
            for k in range(128, N, 128):
                part = part + w[:, k : k + 128]
            parts.append(part)
        part = jnp.concatenate(parts, axis=0).T
        mass[0, r * 4 + g : r * 4 + g + 1, :] = jnp.sum(part, axis=0, keepdims=True)

    def moments(r, g):
        if g % 2:
            return
        spots = [(x + OFFS[g]) % 4, (x + OFFS[g + 1]) % 4]
        blocks = []
        for xx in spots:
            blocks.append(p_v[:, pl.ds(pl.multiple_of(xx * 128, 128), 128)])
            blocks.append(p_v[:, pl.ds(pl.multiple_of(512 + xx * 128, 128), 128)])
        out = jnp.dot(w_v[r % 2], jnp.concatenate(blocks, axis=1), preferred_element_type=F32)
        for k in range(4):
            part = out[:, k * 128 : (k + 1) * 128]
            zero, one = pack(part[:HALF], part[HALF:])
            mp[r, 0, spots[k // 2], k % 2, :, :] = zero
            mp[r, 1, spots[k // 2], k % 2, :, :] = one

    cc = {}

    def send_moments(r, g):
        xx = (x + OFFS[g]) % 4
        cc[r, g] = send(mp.at[r, 1 - c, xx], cr.at[r, xx], cs.at[r, g], crs.at[r, g], sib)

    xc = {}

    def xsend(r, i, src, dst, dev):
        xc[r, i] = send(src, dst, xs.at[r, i], xr.at[r, i], dev)

    x_opp, x_next, x_prev = (x + 2) % 4, (x + 1) % 4, (x + 3) % 4

    def own_centroids(r):
        q = pl.ds(pl.multiple_of((yh * 4 + x) * 128, 128), 128)
        zero, one = pack(c_v[r, :HALF, q].astype(F32), c_v[r, HALF:, q].astype(F32))
        return prior_weight * jnp.where(jnp.full((HALF, 128), c, jnp.int32) == 0, zero, one)

    def sum_cores(r, g):
        ra, hb = SPLIT[r], (HALF - SPLIT[r]) // 2
        rb = 2 * hb
        xx = (x + OFFS[g]) % 4
        for h in range(2):
            sa[r, xx, h, :ra, :] = mp[r, c, xx, h, :ra, :] + cr[r, xx, h, :ra, :]
            sb[r, h, xx, :rb, :] = mp[r, c, xx, h, ra:, :] + cr[r, xx, h, ra:, :]
        if g == 3:
            own = own_centroids(r)
            sa[r, x, yh, :ra, :] += own[:ra]
            sb[r, yh, x, :rb, :] += own[ra:]

    def send_cores(r, g):
        ra, hb = SPLIT[r], (HALF - SPLIT[r]) // 2
        rb = 2 * hb
        if g == 0:
            xsend(r, REL_P, sa.at[r, x_opp, 0, pl.ds(0, ra)], ra_m.at[r, pl.ds(0, ra)], xp)
            xsend(r, REL_M, sa.at[r, x_opp, 1, pl.ds(0, ra)], ra_p.at[r, pl.ds(0, ra)], xm)
        if g == 1:
            xsend(r, PLA_P, sa.at[r, x_next, 1, pl.ds(0, ra)], da_m.at[r, 1, pl.ds(0, ra)], xp)
        if g == 2:
            xsend(r, PLA_M, sa.at[r, x_prev, 0, pl.ds(0, ra)], da_p.at[r, 0, pl.ds(0, ra)], xm)
        xx = (x + OFFS[g]) % 4
        xsend(r, Y_B + g, sb.at[r, 1 - yh, xx, pl.ds(0, rb)], yb.at[r, xx, pl.ds(0, rb)], y2)

    def aug_a(r):
        ra, hb = SPLIT[r], (HALF - SPLIT[r]) // 2
        rb = 2 * hb
        xc[r, REL_P].wait_recv()
        sa[r, x_next, 0, :ra, :] += ra_m[r, :ra]
        xsend(r, AUG_P, sa.at[r, x_next, 0, pl.ds(0, ra)], da_m.at[r, 0, pl.ds(0, ra)], xp)
        xc[r, REL_M].wait_recv()
        sa[r, x_prev, 1, :ra, :] += ra_p[r, :ra]
        xsend(r, AUG_M, sa.at[r, x_prev, 1, pl.ds(0, ra)], da_p.at[r, 1, pl.ds(0, ra)], xm)

    def rel_b(r):
        ra, hb = SPLIT[r], (HALF - SPLIT[r]) // 2
        rb = 2 * hb
        xc[r, Y_B].wait_recv()
        sb[r, yh, x_opp, :rb, :] += yb[r, x_opp, :rb]
        xsend(r, BREL_P, sb.at[r, yh, x_opp, pl.ds(0, hb)], rb_m.at[r, pl.ds(0, hb)], xp)
        xsend(r, BREL_M, sb.at[r, yh, x_opp, pl.ds(hb, hb)], rb_p.at[r, pl.ds(0, hb)], xm)
        xc[r, Y_B + 1].wait_recv()
        sb[r, yh, x_next, :rb, :] += yb[r, x_next, :rb]
        xsend(r, BPLA_P, sb.at[r, yh, x_next, pl.ds(hb, hb)], db_m.at[r, pl.ds(hb, hb)], xp)
        xc[r, Y_B + 2].wait_recv()
        sb[r, yh, x_prev, :rb, :] += yb[r, x_prev, :rb]
        xsend(r, BPLA_M, sb.at[r, yh, x_prev, pl.ds(0, hb)], db_p.at[r, pl.ds(0, hb)], xm)
        xc[r, Y_B + 3].wait_recv()
        sb[r, yh, x, :rb, :] += yb[r, x, :rb]

    def y_a(r):
        ra, hb = SPLIT[r], (HALF - SPLIT[r]) // 2
        rb = 2 * hb
        for i in (PLA_P, PLA_M, AUG_P, AUG_M):
            xc[r, i].wait_recv()
        sa[r, x, 1 - yh, :ra, :] += da_m[r, 1 - yh, :ra] + da_p[r, 1 - yh, :ra]
        xsend(r, Y_A, sa.at[r, x, 1 - yh, pl.ds(0, ra)], ya.at[r, pl.ds(0, ra)], y2)
        sa[r, x, yh, :ra, :] += da_m[r, yh, :ra] + da_p[r, yh, :ra]

    def aug_b(r):
        ra, hb = SPLIT[r], (HALF - SPLIT[r]) // 2
        rb = 2 * hb
        xc[r, BREL_P].wait_recv()
        sb[r, yh, x_next, :hb, :] += rb_m[r, :hb]
        xsend(r, BAUG_P, sb.at[r, yh, x_next, pl.ds(0, hb)], db_m.at[r, pl.ds(0, hb)], xp)
        xc[r, BREL_M].wait_recv()
        sb[r, yh, x_prev, hb:rb, :] += rb_p[r, :hb]
        xsend(r, BAUG_M, sb.at[r, yh, x_prev, pl.ds(hb, hb)], db_p.at[r, pl.ds(hb, hb)], xm)

    mc = {}

    def mass_send(i, src, dst, dev):
        mc[i] = send(mass.at[src], mass.at[dst], ms.at[i], mr.at[i], dev)

    def mass_core():
        mass_send(0, 0, 1, sib)
        mc["lt"] = send(lt.at[l], lt.at[l], ls, lr, other)

    def mass_x():
        mc[0].wait_recv()
        mass[2, :, :] = mass[0] + mass[1]
        for j, dev in ((1, xp), (2, x2), (3, xm)):
            mass_send(j, 2, 2 + j, dev)

    def mass_y():
        for j in (1, 2, 3):
            mc[j].wait_recv()
        mass[6, :, :] = mass[2] + mass[3] + mass[4] + mass[5]
        mass_send(4, 6, 7, y2)

    masses = []

    def receive_mass():
        mc[4].wait_recv()
        masses.append(mass[6] + mass[7])
        mc["lt"].wait_recv()
        b_ref[...] = (lt[0] + lt[1]) / 8.0 - math.log(4096)

    def finish(r):
        ra, hb = SPLIT[r], (HALF - SPLIT[r]) // 2
        rb = 2 * hb
        total = masses[0]
        row = [total[r * 4 + i : r * 4 + i + 1, :] + prior_weight for i in range(4)]
        weight = (jnp.concatenate(row[:2], axis=1), jnp.concatenate(row[2:], axis=1))
        for i in (Y_A, BPLA_P, BPLA_M, BAUG_P, BAUG_M):
            xc[r, i].wait_recv()
        high = sa[r, x, yh, :ra] + ya[r, :ra]
        low = sb[r, yh, x, :rb] + db_m[r, :rb] + db_p[r, :rb]
        moved = jnp.concatenate([high, low], axis=0).T
        for i in range(2):
            u_ref[r, :, i * HALF : (i + 1) * HALF] = (moved[i * 64 : i * 64 + 64] / weight[i]).astype(
                jnp.bfloat16
            )

    logits(0)
    pl.semaphore_wait(barrier, len(peers))
    send_stats(0)
    for r in range(1, REPS):
        logits(r)
        send_stats(r)
    loads[1].wait()
    steps = [(r, g) for r in range(REPS) for g in range(4)]
    stages = {"aug_a": aug_a, "rel_b": rel_b, "y_a": y_a, "aug_b": aug_b, "finish": finish}
    for i in range(len(steps) + LAG):
        late = steps[i - LAG] if i >= LAG else None
        if i < len(steps):
            r, g = steps[i]
            if g == 0:
                scale(r)
                for k in range(4):
                    weights(r, k)
            moments(r, g)
            send_moments(r, g)
        if late:
            cc[late].wait_recv()
            sum_cores(*late)
        if late:
            send_cores(*late)
        if i == 12:
            mass_core()
        if i == 15:
            mass_x()
        for name, r in EARLY.get(i, ()):
            stages[name](r)
    for name, r in LATE:
        if name == "mass_y":
            mass_y()
        elif name == "mass":
            receive_mass()
        else:
            stages[name](r)
    for copy in sent:
        copy.wait_send()


def shards(points, centroids, counts):
    dma = pltpu.SemaphoreType.DMA
    packed, bagged = pl.pallas_call(
        kernel,
        out_shape=(
            pltpu.VMEM((REPS, 64, NK), jnp.bfloat16),
            pltpu.VMEM((1, N), F32),
        ),
        in_specs=[pl.BlockSpec(memory_space=pl.ANY)] * 3,
        out_specs=[pl.BlockSpec(memory_space=pltpu.VMEM)] * 2,
        scratch_shapes=[
            pltpu.VMEM((N, D), jnp.bfloat16),
            pltpu.VMEM((REPS, NK, D), jnp.bfloat16),
            pltpu.VMEM((REPS, N), jnp.int32),
            pltpu.VMEM((REPS, NK, N), F32),
            pltpu.VMEM((2, NK, N), jnp.bfloat16),
            pltpu.VMEM((NK, 128), F32),
            pltpu.VMEM((REPS, 1, N), F32),
            pltpu.VMEM((REPS, 8, 2, N), F32),
            pltpu.VMEM((REPS, 2, 4, 2, HALF, 128), F32),
            pltpu.VMEM((REPS, 4, 2, HALF, 128), F32),
            pltpu.VMEM((REPS, 4, 2, RA, 128), F32),
            pltpu.VMEM((REPS, 2, 4, RB, 128), F32),
            pltpu.VMEM((REPS, RA, 128), F32),
            pltpu.VMEM((REPS, RA, 128), F32),
            pltpu.VMEM((REPS, 2, RA, 128), F32),
            pltpu.VMEM((REPS, 2, RA, 128), F32),
            pltpu.VMEM((REPS, RA, 128), F32),
            pltpu.VMEM((REPS, 4, RB, 128), F32),
            pltpu.VMEM((REPS, HB, 128), F32),
            pltpu.VMEM((REPS, HB, 128), F32),
            pltpu.VMEM((REPS, RB, 128), F32),
            pltpu.VMEM((REPS, RB, 128), F32),
            pltpu.VMEM((8, 4 * REPS, 128), F32),
            pltpu.VMEM((2, 1, N), F32),
            dma((2 + REPS,)),
            dma((REPS, 8)),
            dma((REPS, 8)),
            dma((REPS, 4)),
            dma((REPS, 4)),
            dma((REPS, EXCHANGES)),
            dma((REPS, EXCHANGES)),
            dma((5,)),
            dma((5,)),
            dma,
            dma,
        ],
        compiler_params=pltpu.CompilerParams(
            collective_id=0, has_side_effects=True, vmem_limit_bytes=56 * 1024 * 1024
        ),
    )(points, centroids, counts)
    return packed.transpose(0, 2, 1), bagged.reshape(N)


def solution(mesh):
    return jax.shard_map(
        shards,
        mesh=mesh,
        in_specs=(P("dp", None), P("rep", "cent", None), P("rep", "dp")),
        out_specs=(P("rep", "cent", "dp"), P("dp")),
        check_vma=False,
    )
```
